32 devices in a mesh: lat: 4 (over y, x), lon: 8 (over z, core).
Axes of the slice: x: 2, y: 2, z: 4, core: 2. Of those that a mesh axis runs over, the one named last changes fastest.
Arguments:
- adjoint: float32 [16, 24, 64, 1024], P(None, None, 'lat', 'lon'), may hold values from -6 to 6
- courant: float32 [2, 24, 64, 1024], P(None, None, 'lat', 'lon'), may hold values from -0.35 to 0.35
- vert_diff: float32 [24], replicated, may hold values from 0.005 to 0.05
- kernel: float32 [24, 65536], P(None, ('lat', 'lon')), may hold values from 0.1 to 1
- innovation: float32 [65536], P(('lat', 'lon')), may hold values from -6 to 6
- sound_col: int32 [65536], P(('lat', 'lon')), may hold values from 0 to 65535, as said below
- sound_count: int32 [32], P(('lat', 'lon')), may hold values from 1024 to 2048, as said below
Outputs:
- adjoint_out: float32 [16, 24, 64, 1024], P(None, None, 'lat', 'lon')
The draws below stay inside these ranges and needn't reach their ends.
Inputs may be any that keep to these rules, and one draw needn't show every extreme that they name: `sound_col`: of one device's slots, at most 128 go to grid columns of any one tile of 16 x 128 cells, and in every draw some device sends exactly 128 live soundings to one tile. `sound_count`: device 0 has all its slots live in every draw.
All inputs are finite; a program needn't handle non-finite values.
Results may differ from the reference program's by a relative error of at most 0.00002.
Values sent between devices are 32-bit elements; how exact they have to be, the bound alone decides.
A program may use at most 128 MiB of HBM per device.

```python
import math
import jax
import jax.numpy as jnp

TR = 16
LEV = 24
CLAT = 16
CLON = 128
SND_DEV = 2048
SEG = 128
NLAT = 64
NLON = 1024
SND_ALL = 65536
N_LAT = 4
N_LON = 8


def draw_sound_col(key, part):
    key = jax.random.fold_in(key, 11)
    keys = jax.random.split(key, 4)
    ndev = N_LAT * N_LON
    groups = ndev // 2
    perm_keys = jax.random.split(keys[0], ndev)
    perm = jax.vmap(lambda k: jax.random.permutation(k, ndev))(perm_keys).astype(jnp.int32)
    cutoff = jax.random.randint(keys[1], (ndev, groups), 0, SEG + 1)
    cutoff = cutoff.at[:, 0].set(SEG)
    within = jnp.arange(SEG, dtype=jnp.int32)
    tiles = jnp.where(within[None, None, :] < cutoff[:, :, None], perm[:, :groups, None], perm[:, groups:, None])
    lat_tile = tiles // N_LON
    lon_tile = tiles % N_LON
    lat_cell = jax.random.randint(keys[2], (ndev, groups, SEG), 0, CLAT)
    lon_cell = jax.random.randint(keys[3], (ndev, groups, SEG), 0, CLON)
    column = (lat_tile * CLAT + lat_cell) * (CLON * N_LON) + lon_tile * CLON + lon_cell
    return column.reshape(-1).astype(jnp.int32)


def draw_sound_count(key, part):
    key = jax.random.fold_in(key, 12)
    ndev = N_LAT * N_LON
    counts = jax.random.randint(key, (ndev,), SND_DEV // 2, SND_DEV + 1)
    return counts.at[0].set(SND_DEV).astype(jnp.int32)


def levels(key, shape, cuts, least, top_value):
    def one(dim, shards_of):
        heights = jax.random.uniform(jax.random.fold_in(jax.random.fold_in(key, 6), dim), (shards_of,), jnp.float32, least / len(cuts), top_value / len(cuts))
        return jnp.repeat(jnp.exp(heights), shape[dim] // shards_of).reshape((-1,) + (1,) * (len(shape) - dim - 1))

    gain = one(*cuts[0])
    for cut in cuts[1:]:
        gain = gain * one(*cut)
    return gain


def noise(rng, extent, spread, most, pieces=(), kind=jnp.bfloat16):
    values = spread * jax.random.normal(rng, extent, jnp.float32)
    if pieces:
        values = values * levels(rng, extent, pieces, -0.22, 0.18)
    return jnp.clip(values, -most, most).astype(kind)


def setup_inputs(seed: int = 0) -> dict:
    seeds = jax.random.split(jax.random.key(seed), 8)
    adjoint = noise(seeds[0], (TR, LEV, NLAT, NLON), 1.0, 6.0, ((2, 4), (3, 8)), jnp.float32)
    courant = jnp.clip(jax.random.uniform(seeds[1], (2, LEV, NLAT, NLON), jnp.float32, -0.35, 0.35) * levels(seeds[1], (2, LEV, NLAT, NLON), ((2, 4), (3, 8)), -0.4, 0.0), -0.35, 0.35)
    vert_diff = jnp.clip(jnp.exp(jax.random.uniform(seeds[2], (LEV,), jnp.float32, math.log(0.005), math.log(0.05))), 0.005, 0.05)
    kernel = jnp.clip(jnp.exp(math.log(1.0) - 2.3025851 * jax.random.uniform(seeds[3], (LEV, SND_ALL), jnp.float32) ** levels(seeds[3], (LEV, SND_ALL), ((1, 32),), -0.2, 0.2)), 0.1, 1.0)
    innovation = noise(seeds[4], (SND_ALL,), 1.0, 6.0, ((0, 32),), jnp.float32)
    sound_col = draw_sound_col(jax.random.fold_in(seeds[7], 71), 0)
    sound_count = draw_sound_count(jax.random.fold_in(seeds[7], 71), 0)
    return {"adjoint": adjoint, "courant": courant, "vert_diff": vert_diff, "kernel": kernel, "innovation": innovation, "sound_col": sound_col, "sound_count": sound_count}


def extend(field):
    wide = jnp.concatenate([field[..., -1:], field, field[..., :1]], axis=-1)
    zero = jnp.zeros(wide.shape[:-2] + (1, wide.shape[-1]), jnp.float32)
    return jnp.concatenate([zero, wide, zero], axis=-2)


def advance(padded, winds, vert_diff):
    centre = padded[:, :, 1:-1, 1:-1]
    north = padded[:, :, 2:, 1:-1]
    south = padded[:, :, :-2, 1:-1]
    east = padded[:, :, 1:-1, 2:]
    west = padded[:, :, 1:-1, :-2]
    upper = jnp.concatenate([centre[:, 1:], centre[:, -1:]], axis=1)
    lower = jnp.concatenate([centre[:, :1], centre[:, :-1]], axis=1)
    along = winds[0]
    across = winds[1]
    result = centre + jnp.maximum(along, 0.0) * (east - centre) + jnp.maximum(-along, 0.0) * (west - centre)
    result = result + jnp.maximum(across, 0.0) * (north - centre) + jnp.maximum(-across, 0.0) * (south - centre)
    result = result + 0.05 * (east + west + north + south - 4.0 * centre)
    return result + vert_diff[:, None, None] * (upper + lower - 2.0 * centre)


def reference(adjoint, courant, vert_diff, kernel, innovation, sound_col, sound_count):
    total = sound_col.shape[0]
    slot = jnp.arange(total, dtype=jnp.int32)
    owner = slot // SND_DEV
    live = (slot % SND_DEV) < sound_count[owner]
    ncell = NLAT * NLON
    target = jnp.where(live, sound_col, ncell).astype(jnp.int32)
    payload = kernel * innovation[None, :]
    forcing = jnp.zeros((LEV, ncell), jnp.float32).at[:, target].add(payload, mode="drop")
    forcing = forcing.reshape(LEV, NLAT, NLON)
    middle = advance(extend(adjoint), courant, vert_diff) + forcing[None]
    return advance(extend(middle), courant, vert_diff)
```

```python
import functools

import jax
import jax.numpy as jnp
from jax import lax
from jax.experimental import pallas as pl
from jax.experimental.pallas import tpu as pltpu
from jax.sharding import PartitionSpec as P

MESH = pl.DeviceIdType.MESH
F32 = jnp.float32
BF16 = jnp.bfloat16
GROUP = 4
BLOCK = 8
WIDE = 128
PAY = 32
TOP = 8


def kernel_body(
    lat_n, lon_n, tracers, levels, rows,
    adj, cour, kern, vd, count, innov, cols,
    out, sf,
    q0, q1, fq, wind, coef, kbuf, pbuf, send, recv, a_hi, a_lo, b_hi, b_lo,
    rank_hot, tile_ref, edge, edge_e, edge_w, halo, fedge, fedge_e, fedge_w, obuf,
    load_sem, row_send, row_recv, col_send, col_recv, pay_send, pay_recv,
    f_send, f_recv, out_sem, own_sem,
):
    la = lax.axis_index("lat")
    lo = lax.axis_index("lon")
    me = la * lon_n + lo
    total = lat_n * lon_n
    chunks = tracers // GROUP
    parts = levels // BLOCK
    slots = kern.shape[1]
    pieces = slots // WIDE
    east = lax.rem(lo + 1, lon_n)
    west = lax.rem(lo + lon_n - 1, lon_n)

    barrier = pltpu.get_barrier_semaphore()

    @pl.loop(1, total)
    def _(i):
        p = lax.rem(me + i, total)
        pl.semaphore_signal(
            barrier, inc=1, device_id=(p // lon_n, lax.rem(p, lon_n)), device_id_type=MESH
        )

    kload = pltpu.make_async_copy(kern, kbuf, load_sem.at[0])
    kload.start()
    loads = []
    for g in range(chunks):
        loads.append(
            pltpu.make_async_copy(
                adj.at[pl.ds(g * GROUP, GROUP)],
                q0.at[pl.ds(g * GROUP, GROUP), :, pl.ds(TOP, rows), :],
                load_sem.at[2 + g],
            )
        )
        loads[-1].start()
    wload = pltpu.make_async_copy(cour, wind, load_sem.at[1])
    wload.start()

    col = cols[...]
    grid_cols = lon_n * 128
    grid_row = col // grid_cols
    grid_col = col - grid_row * grid_cols
    tile = (grid_row // rows) * lon_n + grid_col // 128
    cell_row = lax.rem(grid_row, rows)
    cell_col = lax.rem(grid_col, 128)
    slot = (
        lax.broadcasted_iota(jnp.int32, col.shape, 0) * 128
        + lax.broadcasted_iota(jnp.int32, col.shape, 1)
    )
    tile = jnp.where(slot < count[0], tile, -1)
    tile_ref[...] = tile
    earlier = lax.broadcasted_iota(jnp.int32, (2 * WIDE, WIDE), 0)
    later = lax.broadcasted_iota(jnp.int32, (2 * WIDE, WIDE), 1)
    adder = jnp.where((earlier <= later) | (earlier >= WIDE), 1.0, 0.0).astype(BF16)
    ids = lax.broadcasted_iota(jnp.int32, (total, WIDE), 0)
    ranks = lax.broadcasted_iota(jnp.int32, (WIDE, WIDE), 0)
    seen = jnp.zeros((total, WIDE), F32)
    for c in range(pieces):
        hot = jnp.where(ids == tile[c : c + 1, :], 1.0, 0.0)
        both = jnp.concatenate([hot.astype(BF16), seen.astype(BF16)], axis=1)
        before = jnp.dot(both, adder, preferred_element_type=F32)
        rank = jnp.sum(hot * before, axis=0, keepdims=True).astype(jnp.int32) - 1
        rank_hot[:, c * WIDE : (c + 1) * WIDE] = jnp.where(ranks == rank, 1.0, 0.0).astype(BF16)
        seen = seen + hot

    kload.wait()
    for c in range(pieces):
        spot = pl.ds(c * WIDE, WIDE)
        pbuf[0:levels, spot] = kbuf[:, spot] * innov[c : c + 1, :]
        index = lax.broadcasted_iota(jnp.int32, (PAY - levels, WIDE), 0)
        pbuf[levels:PAY, spot] = jnp.where(
            index == 0,
            cell_row[c : c + 1, :].astype(F32),
            jnp.where(index == 1, cell_col[c : c + 1, :].astype(F32), 0.0),
        )

    pl.semaphore_wait(barrier, total - 1)

    def row_copy(field, g, side, start):
        at = pl.ds(g * GROUP, GROUP)
        if side == 0:
            src, dst, to = TOP + rows - 1, TOP - 1, (la + 1, lo)
        else:
            src, dst, to = TOP, TOP + rows, (la - 1, lo)
        k = 0 if field is q0 else 1
        return pltpu.make_async_remote_copy(
            src_ref=field.at[at, :, src, :],
            dst_ref=field.at[at, :, dst, :],
            send_sem=row_send.at[k, side, g],
            recv_sem=row_recv.at[k, side, g],
            device_id=to,
            device_id_type=MESH,
        )

    has_north = la < lat_n - 1
    has_south = la > 0

    def send_rows(field, g):
        @pl.when(has_north)
        def _():
            row_copy(field, g, 0, True).start()

        @pl.when(has_south)
        def _():
            row_copy(field, g, 1, True).start()

    def arrived_rows(field, g):
        @pl.when(has_south)
        def _():
            row_copy(field, g, 0, True).wait_recv()

        @pl.when(has_north)
        def _():
            row_copy(field, g, 1, True).wait_recv()

    def sent_rows(field, g):
        @pl.when(has_north)
        def _():
            row_copy(field, g, 0, True).wait_send()

        @pl.when(has_south)
        def _():
            row_copy(field, g, 1, True).wait_send()

    for field in (q0, q1):
        @pl.when(la == 0)
        def _():
            @pl.loop(0, tracers)
            def _(t):
                field[t, :, 0:TOP, :] = jnp.zeros((levels, TOP, 128), F32)

        @pl.when(la == lat_n - 1)
        def _():
            @pl.loop(0, tracers)
            def _(t):
                field[t, :, TOP + rows :, :] = jnp.zeros((levels, TOP, 128), F32)

    @pl.when(la == 0)
    def _():
        fq[:, 0:TOP, :] = jnp.zeros((levels, TOP, 128), F32)

    @pl.when(la == lat_n - 1)
    def _():
        fq[:, TOP + rows :, :] = jnp.zeros((levels, TOP, 128), F32)

    for g in range(chunks):
        loads[g].wait()
        send_rows(q0, g)

    def pay_copy(p, src):
        return pltpu.make_async_remote_copy(
            src_ref=send.at[p],
            dst_ref=recv.at[src],
            send_sem=pay_send.at[p],
            recv_sem=pay_recv.at[src],
            device_id=(p // lon_n, lax.rem(p, lon_n)),
            device_id_type=MESH,
        )

    own = pltpu.make_async_copy(send.at[me], recv.at[me], own_sem.at[0])

    @pl.loop(0, lat_n)
    def _(step):
        row = lax.rem(la + 1 + step, lat_n)

        for c in range(pieces):
            spot = pl.ds(c * WIDE, WIDE)
            block = pbuf[:, spot]
            hi = block.astype(BF16).astype(F32)
            low = block - hi
            where_to = jnp.broadcast_to(tile_ref[c : c + 1, :], (PAY, WIDE)) - row * lon_n
            for d in range(lon_n):
                mine = where_to == d
                a_hi[d * PAY : (d + 1) * PAY, spot] = jnp.where(mine, hi, 0.0).astype(BF16)
                a_lo[d * PAY : (d + 1) * PAY, spot] = jnp.where(mine, low, 0.0).astype(BF16)
        contract = (((1,), (1,)), ((), ()))
        packed = lax.dot_general(
            a_hi[...], rank_hot[...], contract, preferred_element_type=F32
        ) + lax.dot_general(a_lo[...], rank_hot[...], contract, preferred_element_type=F32)
        send[pl.ds(row * lon_n, lon_n)] = packed.reshape(lon_n, PAY, WIDE)

        @pl.loop(0, lon_n)
        def _(j):
            p = row * lon_n + j

            @pl.when(p != me)
            def _():
                pay_copy(p, me).start()

    own.start()

    lane = lax.broadcasted_iota(jnp.int32, (rows, 128), 1)
    first = lane == 0
    last = lane == 127

    def col_copy(k, g, side):
        return pltpu.make_async_remote_copy(
            src_ref=edge.at[k, g],
            dst_ref=(edge_w if side == 0 else edge_e).at[k, g],
            send_sem=col_send.at[k, side, g],
            recv_sem=col_recv.at[k, side, g],
            device_id=(la, east if side == 0 else west),
            device_id_type=MESH,
        )

    def gather_edges(read, count_blocks):
        lanes = lax.broadcasted_iota(jnp.int32, (BLOCK * rows, 128), 1)
        packed = jnp.zeros((BLOCK * rows, 128), F32)
        for k in range(count_blocks):
            block = read(k).reshape(BLOCK * rows, 128)
            packed = jnp.where(lanes // 2 == k, pltpu.roll(block, (1 + 2 * k) % 128, 1), packed)
        return packed.T

    def spread(from_e, from_w):
        tall = from_e.shape[0]
        odd = lax.rem(lax.broadcasted_iota(jnp.int32, (tall, 128), 0), 2) == 1
        mixed = jnp.where(odd, pltpu.roll(from_w, 1, 0), pltpu.roll(from_e, tall - 1, 0))
        if tall < 128:
            mixed = jnp.concatenate([mixed, jnp.zeros((128 - tall, 128), F32)], axis=0)
        return mixed.T

    def send_cols(field, k, g):
        def read(b):
            return field[
                g * GROUP + b // parts,
                pl.ds((b % parts) * BLOCK, BLOCK),
                pl.ds(TOP, rows),
                :,
            ]

        edge[k, g] = gather_edges(read, GROUP * parts)[: edge.shape[2]]
        for side in (0, 1):
            col_copy(k, g, side).start()

    @pl.loop(0, chunks)
    def _(g):
        send_cols(q0, 0, g)

    wload.wait()

    @pl.loop(0, levels)
    def _(l):
        u = wind[0, l]
        v = wind[1, l]
        coef[0, l] = 0.8 - jnp.abs(u) - jnp.abs(v) - 2.0 * vd[l]
        coef[1, l] = jnp.maximum(u, 0.0) + 0.05
        coef[2, l] = jnp.maximum(-u, 0.0) + 0.05
        coef[3, l] = jnp.maximum(v, 0.0) + 0.05
        coef[4, l] = jnp.maximum(-v, 0.0) + 0.05

    def stencil(read, l, edges, k, cs):
        q = read(l, TOP)
        beside = pltpu.roll(edges, 127 - 2 * k, 1)
        e = jnp.where(last, beside, pltpu.roll(q, 127, 1))
        w = jnp.where(first, beside, pltpu.roll(q, 1, 1))
        n = read(l, TOP + 1)
        s = read(l, TOP - 1)
        up = read(jnp.minimum(l + 1, levels - 1), TOP)
        down = read(jnp.maximum(l - 1, 0), TOP)
        c0, ce, cw, cn, cs_, cv = cs
        return (c0 * q + ce * e) + (cw * w + cn * n) + (cs_ * s + cv * (up + down))

    def coefs(l):
        return tuple(coef[i, l] for i in range(5)) + (vd[l],)

    def advance(field, k, g, write):
        arrived_rows(field, g)
        for side in (0, 1):
            col_copy(k, g, side).wait_recv()
        halo[...] = spread(edge_e[k, g], edge_w[k, g])
        for part in range(parts):
            @pl.loop(0, BLOCK)
            def _(j):
                l = part * BLOCK + j
                cs = coefs(l)
                edges = halo[pl.ds(pl.multiple_of(j * rows, rows), rows), :]
                for i in range(GROUP):
                    t = g * GROUP + i

                    def read(level, r):
                        return field[t, level, pl.ds(r, rows), :]

                    write(i, t, l, stencil(read, l, edges, i * parts + part, cs))

    @pl.loop(0, chunks)
    def _(g):
        def write(i, t, l, value):
            q1[t, l, TOP : TOP + rows, :] = value

        advance(q0, 0, g, write)
        send_rows(q1, g)
        send_cols(q1, 1, g)

    def out_copy(g):
        at = pl.ds(g * GROUP, GROUP)
        return pltpu.make_async_copy(obuf.at[at], out.at[at], out_sem.at[g])

    @pl.loop(0, chunks)
    def _(g):
        def write(i, t, l, value):
            obuf[t, l] = value

        advance(q1, 1, g, write)
        out_copy(g).start()

    own.wait()
    tile_rows = lax.broadcasted_iota(jnp.int32, (rows, WIDE), 0)
    fq[:, TOP : TOP + rows, :] = jnp.zeros((levels, rows, 128), F32)

    @pl.loop(0, lat_n)
    def _(step):
        source_row = lax.rem(la + lat_n - 1 - step + lat_n, lat_n)

        @pl.loop(0, lon_n)
        def _(j):
            src = source_row * lon_n + j

            @pl.when(src != me)
            def _():
                pay_copy(src, src).wait_recv()

        columns = []
        for j in range(lon_n):
            block = recv[source_row * lon_n + j]
            hi = block.astype(BF16).astype(F32)
            low = block - hi
            here = tile_rows == block[levels : levels + 1, :].astype(jnp.int32)
            spot = pl.ds(j * WIDE, WIDE)
            for l in range(levels):
                b_hi[l * rows : (l + 1) * rows, spot] = jnp.where(
                    here, hi[l : l + 1, :], 0.0
                ).astype(BF16)
                b_lo[l * rows : (l + 1) * rows, spot] = jnp.where(
                    here, low[l : l + 1, :], 0.0
                ).astype(BF16)
            columns.append(
                jnp.where(
                    ranks == block[levels + 1 : levels + 2, :].astype(jnp.int32), 1.0, 0.0
                ).astype(BF16)
            )
        hot = jnp.concatenate(columns, axis=1)
        contract = (((1,), (1,)), ((), ()))
        part = lax.dot_general(
            b_hi[...], hot, contract, preferred_element_type=F32
        ) + lax.dot_general(b_lo[...], hot, contract, preferred_element_type=F32)
        fq[:, TOP : TOP + rows, :] += part.reshape(levels, rows, 128)

    def f_rows(side):
        if side == 0:
            src, dst, to = TOP + rows - 1, TOP - 1, (la + 1, lo)
        else:
            src, dst, to = TOP, TOP + rows, (la - 1, lo)
        return pltpu.make_async_remote_copy(
            src_ref=fq.at[:, src, :],
            dst_ref=fq.at[:, dst, :],
            send_sem=f_send.at[side],
            recv_sem=f_recv.at[side],
            device_id=to,
            device_id_type=MESH,
        )

    def f_cols(side):
        return pltpu.make_async_remote_copy(
            src_ref=fedge,
            dst_ref=fedge_w if side == 0 else fedge_e,
            send_sem=f_send.at[2 + side],
            recv_sem=f_recv.at[2 + side],
            device_id=(la, east if side == 0 else west),
            device_id_type=MESH,
        )

    @pl.when(has_north)
    def _():
        f_rows(0).start()

    @pl.when(has_south)
    def _():
        f_rows(1).start()

    fedge[...] = gather_edges(
        lambda b: fq[pl.ds(b * BLOCK, BLOCK), pl.ds(TOP, rows), :], parts
    )[: fedge.shape[0]]
    for side in (0, 1):
        f_cols(side).start()
    for side in (0, 1):
        f_cols(side).wait_recv()

    @pl.when(has_south)
    def _():
        f_rows(0).wait_recv()

    @pl.when(has_north)
    def _():
        f_rows(1).wait_recv()

    halo[...] = spread(fedge_e[...], fedge_w[...])
    for part in range(parts):
        @pl.loop(0, BLOCK)
        def _(j):
            l = part * BLOCK + j

            def read(level, r):
                return fq[level, pl.ds(r, rows), :]

            edges = halo[pl.ds(pl.multiple_of(j * rows, rows), rows), :]
            sf[l] = stencil(read, l, edges, part, coefs(l))

    @pl.loop(0, total)
    def _(p):
        @pl.when(p != me)
        def _():
            pay_copy(p, me).wait_send()

    @pl.loop(0, chunks)
    def _(g):
        for k, field in ((0, q0), (1, q1)):
            sent_rows(field, g)
            for side in (0, 1):
                col_copy(k, g, side).wait_send()
        out_copy(g).wait()

    @pl.when(has_north)
    def _():
        f_rows(0).wait_send()

    @pl.when(has_south)
    def _():
        f_rows(1).wait_send()

    for side in (0, 1):
        f_cols(side).wait_send()


def per_device(adjoint, courant, vert_diff, kernel, innovation, sound_col, sound_count):
    tracers, levels, rows, columns = adjoint.shape
    lat_n = lax.axis_size("lat")
    lon_n = lax.axis_size("lon")
    total = lat_n * lon_n
    slots = sound_col.shape[0]
    chunks = tracers // GROUP
    parts = levels // BLOCK
    assert columns == 128 and rows == 16 and 2 * slots // total <= WIDE
    tall = rows + 2 * TOP
    edge_rows = -(-2 * GROUP * parts // 8) * 8
    vmem = pl.BlockSpec(memory_space=pltpu.VMEM)
    smem = pl.BlockSpec(memory_space=pltpu.SMEM)
    hbm = pl.BlockSpec(memory_space=pl.ANY)
    dma = pltpu.SemaphoreType.DMA
    twice, forced = pl.pallas_call(
        functools.partial(kernel_body, lat_n, lon_n, tracers, levels, rows),
        out_shape=(
            jax.ShapeDtypeStruct(adjoint.shape, F32),
            jax.ShapeDtypeStruct((levels, rows, 128), F32),
        ),
        in_specs=[hbm, hbm, hbm, smem, smem, vmem, vmem],
        out_specs=(hbm, vmem),
        scratch_shapes=[
            pltpu.VMEM((tracers, levels, tall, 128), F32),
            pltpu.VMEM((tracers, levels, tall, 128), F32),
            pltpu.VMEM((levels, tall, 128), F32),
            pltpu.VMEM((2, levels, rows, 128), F32),
            pltpu.VMEM((5, levels, rows, 128), F32),
            pltpu.VMEM((levels, slots), F32),
            pltpu.VMEM((PAY, slots), F32),
            pltpu.VMEM((total, PAY, WIDE), F32),
            pltpu.VMEM((total, PAY, WIDE), F32),
            pltpu.VMEM((lon_n * PAY, slots), BF16),
            pltpu.VMEM((lon_n * PAY, slots), BF16),
            pltpu.VMEM((levels * rows, lon_n * WIDE), BF16),
            pltpu.VMEM((levels * rows, lon_n * WIDE), BF16),
            pltpu.VMEM((WIDE, slots), BF16),
            pltpu.VMEM((slots // 128, 128), jnp.int32),
            pltpu.VMEM((2, chunks, edge_rows, 128), F32),
            pltpu.VMEM((2, chunks, edge_rows, 128), F32),
            pltpu.VMEM((2, chunks, edge_rows, 128), F32),
            pltpu.VMEM((BLOCK * rows, 128), F32),
            pltpu.VMEM((8, 128), F32),
            pltpu.VMEM((8, 128), F32),
            pltpu.VMEM((8, 128), F32),
            pltpu.VMEM(adjoint.shape, F32),
            dma((2 + chunks,)),
            dma((2, 2, chunks)),
            dma((2, 2, chunks)),
            dma((2, 2, chunks)),
            dma((2, 2, chunks)),
            dma((total,)),
            dma((total,)),
            dma((4,)),
            dma((4,)),
            dma((chunks,)),
            dma((1,)),
        ],
        compiler_params=pltpu.CompilerParams(
            collective_id=0, has_side_effects=True, vmem_limit_bytes=48 * 1024 * 1024
        ),
    )(
        adjoint,
        courant,
        kernel,
        vert_diff,
        sound_count,
        innovation.reshape(slots // 128, 128),
        sound_col.reshape(slots // 128, 128),
    )
    return twice + forced[None]


def solution(mesh):
    placed = (
        P(None, None, "lat", "lon"),
        P(None, None, "lat", "lon"),
        P(),
        P(None, ("lat", "lon")),
        P(("lat", "lon")),
        P(("lat", "lon")),
        P(("lat", "lon")),
    )
    return jax.shard_map(
        per_device,
        mesh=mesh,
        in_specs=placed,
        out_specs=P(None, None, "lat", "lon"),
        check_vma=False,
    )
```

```python
import functools

import jax
import jax.numpy as jnp
from jax import lax
from jax.experimental import pallas as pl
from jax.experimental.pallas import tpu as pltpu
from jax.sharding import PartitionSpec as P

MESH = pl.DeviceIdType.MESH
F32 = jnp.float32
BF16 = jnp.bfloat16
GROUP = 4
BLOCK = 8
WIDE = 128
PAY = 32
TOP = 8


def kernel_body(
    lat_n, lon_n, tracers, levels, rows,
    adj, cour, kern, vd, count, innov_hbm, cols_hbm,
    out, sf,
    q0, q1, fq, wind, coef, kbuf, pbuf, send, recv, a_hi, a_lo, b_hi, b_lo,
    rank_hot, tile_ref, edge, edge_e, edge_w, halo, fedge, fedge_e, fedge_w, innov, cols, obuf,
    load_sem, row_send, row_recv, col_send, col_recv, pay_send, pay_recv,
    f_send, f_recv, out_sem, own_sem,
):
    la = lax.axis_index("lat")
    lo = lax.axis_index("lon")
    me = la * lon_n + lo
    total = lat_n * lon_n
    chunks = tracers // GROUP
    parts = levels // BLOCK
    slots = kern.shape[1]
    pieces = slots // WIDE
    east = lax.rem(lo + 1, lon_n)
    west = lax.rem(lo + lon_n - 1, lon_n)

    barrier = pltpu.get_barrier_semaphore()

    @pl.loop(1, total)
    def _(i):
        p = lax.rem(me + i, total)
        pl.semaphore_signal(
            barrier, inc=1, device_id=(p // lon_n, lax.rem(p, lon_n)), device_id_type=MESH
        )

    cload = pltpu.make_async_copy(cols_hbm, cols, load_sem.at[2])
    cload.start()
    iload = pltpu.make_async_copy(innov_hbm, innov, load_sem.at[3])
    iload.start()
    kload = pltpu.make_async_copy(kern, kbuf, load_sem.at[0])
    kload.start()
    loads = []
    for g in range(chunks):
        loads.append(
            pltpu.make_async_copy(
                adj.at[pl.ds(g * GROUP, GROUP)],
                q0.at[pl.ds(g * GROUP, GROUP), :, pl.ds(TOP, rows), :],
                load_sem.at[4 + g],
            )
        )
        loads[-1].start()
    wload = pltpu.make_async_copy(cour, wind, load_sem.at[1])
    wload.start()

    cload.wait()
    col = cols[...]
    grid_cols = lon_n * 128
    grid_row = col // grid_cols
    grid_col = col - grid_row * grid_cols
    tile = (grid_row // rows) * lon_n + grid_col // 128
    cell_row = lax.rem(grid_row, rows)
    cell_col = lax.rem(grid_col, 128)
    slot = (
        lax.broadcasted_iota(jnp.int32, col.shape, 0) * 128
        + lax.broadcasted_iota(jnp.int32, col.shape, 1)
    )
    tile = jnp.where(slot < count[0], tile, -1)
    tile_ref[...] = tile
    earlier = lax.broadcasted_iota(jnp.int32, (2 * WIDE, WIDE), 0)
    later = lax.broadcasted_iota(jnp.int32, (2 * WIDE, WIDE), 1)
    adder = jnp.where((earlier <= later) | (earlier >= WIDE), 1.0, 0.0).astype(BF16)
    ids = lax.broadcasted_iota(jnp.int32, (total, WIDE), 0)
    ranks = lax.broadcasted_iota(jnp.int32, (WIDE, WIDE), 0)
    seen = jnp.zeros((total, WIDE), F32)
    for c in range(pieces):
        hot = jnp.where(ids == tile[c : c + 1, :], 1.0, 0.0)
        both = jnp.concatenate([hot.astype(BF16), seen.astype(BF16)], axis=1)
        before = jnp.dot(both, adder, preferred_element_type=F32)
        rank = jnp.sum(hot * before, axis=0, keepdims=True).astype(jnp.int32) - 1
        rank_hot[:, c * WIDE : (c + 1) * WIDE] = jnp.where(ranks == rank, 1.0, 0.0).astype(BF16)
        seen = seen + hot

    kload.wait()
    iload.wait()
    for c in range(pieces):
        spot = pl.ds(c * WIDE, WIDE)
        pbuf[0:levels, spot] = kbuf[:, spot] * innov[c : c + 1, :]
        index = lax.broadcasted_iota(jnp.int32, (PAY - levels, WIDE), 0)
        pbuf[levels:PAY, spot] = jnp.where(
            index == 0,
            cell_row[c : c + 1, :].astype(F32),
            jnp.where(index == 1, cell_col[c : c + 1, :].astype(F32), 0.0),
        )

    pl.semaphore_wait(barrier, total - 1)

    def row_copy(field, g, side, start):
        at = pl.ds(g * GROUP, GROUP)
        if side == 0:
            src, dst, to = TOP + rows - 1, TOP - 1, (la + 1, lo)
        else:
            src, dst, to = TOP, TOP + rows, (la - 1, lo)
        k = 0 if field is q0 else 1
        return pltpu.make_async_remote_copy(
            src_ref=field.at[at, :, src, :],
            dst_ref=field.at[at, :, dst, :],
            send_sem=row_send.at[k, side, g],
            recv_sem=row_recv.at[k, side, g],
            device_id=to,
            device_id_type=MESH,
        )

    has_north = la < lat_n - 1
    has_south = la > 0

    def send_rows(field, g):
        @pl.when(has_north)
        def _():
            row_copy(field, g, 0, True).start()

        @pl.when(has_south)
        def _():
            row_copy(field, g, 1, True).start()

    def arrived_rows(field, g):
        @pl.when(has_south)
        def _():
            row_copy(field, g, 0, True).wait_recv()

        @pl.when(has_north)
        def _():
            row_copy(field, g, 1, True).wait_recv()

    def sent_rows(field, g):
        @pl.when(has_north)
        def _():
            row_copy(field, g, 0, True).wait_send()

        @pl.when(has_south)
        def _():
            row_copy(field, g, 1, True).wait_send()

    for field in (q0, q1):
        @pl.when(la == 0)
        def _():
            @pl.loop(0, tracers)
            def _(t):
                field[t, :, 0:TOP, :] = jnp.zeros((levels, TOP, 128), F32)

        @pl.when(la == lat_n - 1)
        def _():
            @pl.loop(0, tracers)
            def _(t):
                field[t, :, TOP + rows :, :] = jnp.zeros((levels, TOP, 128), F32)

    @pl.when(la == 0)
    def _():
        fq[:, 0:TOP, :] = jnp.zeros((levels, TOP, 128), F32)

    @pl.when(la == lat_n - 1)
    def _():
        fq[:, TOP + rows :, :] = jnp.zeros((levels, TOP, 128), F32)

    for g in range(chunks):
        loads[g].wait()
        send_rows(q0, g)

    lane = lax.broadcasted_iota(jnp.int32, (rows, 128), 1)
    first = lane == 0
    last = lane == 127

    def col_copy(k, g, side):
        return pltpu.make_async_remote_copy(
            src_ref=edge.at[k, g],
            dst_ref=(edge_w if side == 0 else edge_e).at[k, g],
            send_sem=col_send.at[k, side, g],
            recv_sem=col_recv.at[k, side, g],
            device_id=(la, east if side == 0 else west),
            device_id_type=MESH,
        )

    def gather_edges(read, count_blocks):
        lanes = lax.broadcasted_iota(jnp.int32, (BLOCK * rows, 128), 1)
        packed = jnp.zeros((BLOCK * rows, 128), F32)
        for k in range(count_blocks):
            block = read(k).reshape(BLOCK * rows, 128)
            packed = jnp.where(lanes // 2 == k, pltpu.roll(block, (1 + 2 * k) % 128, 1), packed)
        return packed.T

    def spread(from_e, from_w):
        tall = from_e.shape[0]
        odd = lax.rem(lax.broadcasted_iota(jnp.int32, (tall, 128), 0), 2) == 1
        mixed = jnp.where(odd, pltpu.roll(from_w, 1, 0), pltpu.roll(from_e, tall - 1, 0))
        if tall < 128:
            mixed = jnp.concatenate([mixed, jnp.zeros((128 - tall, 128), F32)], axis=0)
        return mixed.T

    def send_cols(field, k, g):
        def read(b):
            return field[
                g * GROUP + b // parts,
                pl.ds((b % parts) * BLOCK, BLOCK),
                pl.ds(TOP, rows),
                :,
            ]

        edge[k, g] = gather_edges(read, GROUP * parts)[: edge.shape[2]]
        for side in (0, 1):
            col_copy(k, g, side).start()

    @pl.loop(0, chunks)
    def _(g):
        send_cols(q0, 0, g)

    def pay_copy(p, src):
        return pltpu.make_async_remote_copy(
            src_ref=send.at[p],
            dst_ref=recv.at[src],
            send_sem=pay_send.at[p],
            recv_sem=pay_recv.at[src],
            device_id=(p // lon_n, lax.rem(p, lon_n)),
            device_id_type=MESH,
        )

    own = pltpu.make_async_copy(send.at[me], recv.at[me], own_sem.at[0])

    @pl.loop(0, lat_n)
    def _(step):
        row = lax.rem(la + 1 + step, lat_n)

        for c in range(pieces):
            spot = pl.ds(c * WIDE, WIDE)
            block = pbuf[:, spot]
            hi = block.astype(BF16).astype(F32)
            low = block - hi
            where_to = jnp.broadcast_to(tile_ref[c : c + 1, :], (PAY, WIDE)) - row * lon_n
            for d in range(lon_n):
                mine = where_to == d
                a_hi[d * PAY : (d + 1) * PAY, spot] = jnp.where(mine, hi, 0.0).astype(BF16)
                a_lo[d * PAY : (d + 1) * PAY, spot] = jnp.where(mine, low, 0.0).astype(BF16)
        contract = (((1,), (1,)), ((), ()))
        packed = lax.dot_general(
            a_hi[...], rank_hot[...], contract, preferred_element_type=F32
        ) + lax.dot_general(a_lo[...], rank_hot[...], contract, preferred_element_type=F32)
        send[pl.ds(row * lon_n, lon_n)] = packed.reshape(lon_n, PAY, WIDE)

        @pl.loop(0, lon_n)
        def _(j):
            p = row * lon_n + j

            @pl.when(p != me)
            def _():
                pay_copy(p, me).start()

    own.start()

    wload.wait()

    @pl.loop(0, levels, unroll=4)
    def _(l):
        u = wind[0, l]
        v = wind[1, l]
        coef[0, l] = 0.8 - jnp.abs(u) - jnp.abs(v) - 2.0 * vd[l]
        coef[1, l] = jnp.maximum(u, 0.0) + 0.05
        coef[2, l] = jnp.maximum(-u, 0.0) + 0.05
        coef[3, l] = jnp.maximum(v, 0.0) + 0.05
        coef[4, l] = jnp.maximum(-v, 0.0) + 0.05

    def stencil(read, l, edges, k, cs):
        q = read(l, TOP)
        beside = pltpu.roll(edges, 127 - 2 * k, 1)
        e = jnp.where(last, beside, pltpu.roll(q, 127, 1))
        w = jnp.where(first, beside, pltpu.roll(q, 1, 1))
        n = read(l, TOP + 1)
        s = read(l, TOP - 1)
        up = read(min(l + 1, levels - 1) if isinstance(l, int) else jnp.minimum(l + 1, levels - 1), TOP)
        down = read(max(l - 1, 0) if isinstance(l, int) else jnp.maximum(l - 1, 0), TOP)
        c0, ce, cw, cn, cs_, cv = cs
        return (c0 * q + ce * e) + (cw * w + cn * n) + (cs_ * s + cv * (up + down))

    def coefs(l):
        return tuple(coef[i, l] for i in range(5)) + (vd[l],)

    def advance(field, k, g, write):
        arrived_rows(field, g)
        for side in (0, 1):
            col_copy(k, g, side).wait_recv()
        halo[...] = spread(edge_e[k, g], edge_w[k, g])
        for part in range(parts):
            @pl.loop(0, BLOCK // 4)
            def _(pair):
                done = []
                for near in range(4):
                    j = pair * 4 + near
                    l = part * BLOCK + j
                    cs = coefs(l)
                    edges = halo[pl.ds(pl.multiple_of(j * rows, rows), rows), :]
                    for i in range(GROUP):
                        t = g * GROUP + i

                        def read(level, r):
                            return field[t, level, pl.ds(r, rows), :]

                        done.append((i, t, l, stencil(read, l, edges, i * parts + part, cs)))
                for item in done:
                    write(*item)

    @pl.loop(0, chunks)
    def _(g):
        def write(i, t, l, value):
            q1[t, l, TOP : TOP + rows, :] = value

        advance(q0, 0, g, write)
        send_rows(q1, g)
        send_cols(q1, 1, g)

    def out_copy(g):
        at = pl.ds(g * GROUP, GROUP)
        return pltpu.make_async_copy(obuf.at[at], out.at[at], out_sem.at[g])

    @pl.loop(0, chunks)
    def _(g):
        def write(i, t, l, value):
            obuf[t, l] = value

        advance(q1, 1, g, write)
        out_copy(g).start()

    own.wait()
    tile_rows = lax.broadcasted_iota(jnp.int32, (rows, WIDE), 0)
    fq[:, TOP : TOP + rows, :] = jnp.zeros((levels, rows, 128), F32)

    @pl.loop(0, lat_n)
    def _(step):
        source_row = lax.rem(la + lat_n - 1 - step + lat_n, lat_n)

        @pl.loop(0, lon_n)
        def _(j):
            src = source_row * lon_n + j

            @pl.when(src != me)
            def _():
                pay_copy(src, src).wait_recv()

        columns = []
        for j in range(lon_n):
            block = recv[source_row * lon_n + j]
            hi = block.astype(BF16).astype(F32)
            low = block - hi
            here = tile_rows == block[levels : levels + 1, :].astype(jnp.int32)
            spot = pl.ds(j * WIDE, WIDE)
            for l in range(levels):
                b_hi[l * rows : (l + 1) * rows, spot] = jnp.where(
                    here, hi[l : l + 1, :], 0.0
                ).astype(BF16)
                b_lo[l * rows : (l + 1) * rows, spot] = jnp.where(
                    here, low[l : l + 1, :], 0.0
                ).astype(BF16)
            columns.append(
                jnp.where(
                    ranks == block[levels + 1 : levels + 2, :].astype(jnp.int32), 1.0, 0.0
                ).astype(BF16)
            )
        hot = jnp.concatenate(columns, axis=1)
        contract = (((1,), (1,)), ((), ()))
        part = lax.dot_general(
            b_hi[...], hot, contract, preferred_element_type=F32
        ) + lax.dot_general(b_lo[...], hot, contract, preferred_element_type=F32)
        fq[:, TOP : TOP + rows, :] += part.reshape(levels, rows, 128)

    def f_rows(side):
        if side == 0:
            src, dst, to = TOP + rows - 1, TOP - 1, (la + 1, lo)
        else:
            src, dst, to = TOP, TOP + rows, (la - 1, lo)
        return pltpu.make_async_remote_copy(
            src_ref=fq.at[:, src, :],
            dst_ref=fq.at[:, dst, :],
            send_sem=f_send.at[side],
            recv_sem=f_recv.at[side],
            device_id=to,
            device_id_type=MESH,
        )

    def f_cols(side):
        return pltpu.make_async_remote_copy(
            src_ref=fedge,
            dst_ref=fedge_w if side == 0 else fedge_e,
            send_sem=f_send.at[2 + side],
            recv_sem=f_recv.at[2 + side],
            device_id=(la, east if side == 0 else west),
            device_id_type=MESH,
        )

    @pl.when(has_north)
    def _():
        f_rows(0).start()

    @pl.when(has_south)
    def _():
        f_rows(1).start()

    fedge[...] = gather_edges(
        lambda b: fq[pl.ds(b * BLOCK, BLOCK), pl.ds(TOP, rows), :], parts
    )[: fedge.shape[0]]
    for side in (0, 1):
        f_cols(side).start()
    for side in (0, 1):
        f_cols(side).wait_recv()

    @pl.when(has_south)
    def _():
        f_rows(0).wait_recv()

    @pl.when(has_north)
    def _():
        f_rows(1).wait_recv()

    halo[...] = spread(fedge_e[...], fedge_w[...])
    for part in range(parts):
        done = []
        for j in range(BLOCK):
            l = part * BLOCK + j

            def read(level, r):
                return fq[level, pl.ds(r, rows), :]

            edges = halo[j * rows : (j + 1) * rows, :]
            done.append((l, stencil(read, l, edges, part, coefs(l))))
        for l, value in done:
            sf[l] = value

    @pl.loop(0, total)
    def _(p):
        @pl.when(p != me)
        def _():
            pay_copy(p, me).wait_send()

    @pl.loop(0, chunks)
    def _(g):
        for k, field in ((0, q0), (1, q1)):
            sent_rows(field, g)
            for side in (0, 1):
                col_copy(k, g, side).wait_send()
        out_copy(g).wait()

    @pl.when(has_north)
    def _():
        f_rows(0).wait_send()

    @pl.when(has_south)
    def _():
        f_rows(1).wait_send()

    for side in (0, 1):
        f_cols(side).wait_send()


def per_device(adjoint, courant, vert_diff, kernel, innovation, sound_col, sound_count):
    tracers, levels, rows, columns = adjoint.shape
    lat_n = lax.axis_size("lat")
    lon_n = lax.axis_size("lon")
    total = lat_n * lon_n
    slots = sound_col.shape[0]
    chunks = tracers // GROUP
    parts = levels // BLOCK
    assert columns == 128 and rows == 16 and 2 * slots // total <= WIDE
    tall = rows + 2 * TOP
    edge_rows = -(-2 * GROUP * parts // 8) * 8
    vmem = pl.BlockSpec(memory_space=pltpu.VMEM)
    smem = pl.BlockSpec(memory_space=pltpu.SMEM)
    far = pl.BlockSpec(memory_space=pltpu.HBM)
    dma = pltpu.SemaphoreType.DMA
    twice, forced = pl.pallas_call(
        functools.partial(kernel_body, lat_n, lon_n, tracers, levels, rows),
        out_shape=(
            jax.ShapeDtypeStruct(adjoint.shape, F32),
            jax.ShapeDtypeStruct((levels, rows, 128), F32),
        ),
        in_specs=[far, far, far, smem, smem, far, far],
        out_specs=(far, vmem),
        scratch_shapes=[
            pltpu.VMEM((tracers, levels, tall, 128), F32),
            pltpu.VMEM((tracers, levels, tall, 128), F32),
            pltpu.VMEM((levels, tall, 128), F32),
            pltpu.VMEM((2, levels, rows, 128), F32),
            pltpu.VMEM((5, levels, rows, 128), F32),
            pltpu.VMEM((levels, slots), F32),
            pltpu.VMEM((PAY, slots), F32),
            pltpu.VMEM((total, PAY, WIDE), F32),
            pltpu.VMEM((total, PAY, WIDE), F32),
            pltpu.VMEM((lon_n * PAY, slots), BF16),
            pltpu.VMEM((lon_n * PAY, slots), BF16),
            pltpu.VMEM((levels * rows, lon_n * WIDE), BF16),
            pltpu.VMEM((levels * rows, lon_n * WIDE), BF16),
            pltpu.VMEM((WIDE, slots), BF16),
            pltpu.VMEM((slots // 128, 128), jnp.int32),
            pltpu.VMEM((2, chunks, edge_rows, 128), F32),
            pltpu.VMEM((2, chunks, edge_rows, 128), F32),
            pltpu.VMEM((2, chunks, edge_rows, 128), F32),
            pltpu.VMEM((BLOCK * rows, 128), F32),
            pltpu.VMEM((8, 128), F32),
            pltpu.VMEM((8, 128), F32),
            pltpu.VMEM((8, 128), F32),
            pltpu.VMEM((slots // 128, 128), F32),
            pltpu.VMEM((slots // 128, 128), jnp.int32),
            pltpu.VMEM(adjoint.shape, F32),
            dma((4 + chunks,)),
            dma((2, 2, chunks)),
            dma((2, 2, chunks)),
            dma((2, 2, chunks)),
            dma((2, 2, chunks)),
            dma((total,)),
            dma((total,)),
            dma((4,)),
            dma((4,)),
            dma((chunks,)),
            dma((1,)),
        ],
        compiler_params=pltpu.CompilerParams(
            collective_id=0, has_side_effects=True, vmem_limit_bytes=62 * 1024 * 1024
        ),
    )(
        adjoint,
        courant,
        kernel,
        vert_diff,
        sound_count,
        innovation.reshape(slots // 128, 128),
        sound_col.reshape(slots // 128, 128),
    )
    return twice + forced[None]


def solution(mesh):
    placed = (
        P(None, None, "lat", "lon"),
        P(None, None, "lat", "lon"),
        P(),
        P(None, ("lat", "lon")),
        P(("lat", "lon")),
        P(("lat", "lon")),
        P(("lat", "lon")),
    )
    return jax.shard_map(
        per_device,
        mesh=mesh,
        in_specs=placed,
        out_specs=P(None, None, "lat", "lon"),
        check_vma=False,
    )
```

```python
import functools

import jax
import jax.numpy as jnp
from jax import lax
from jax.experimental import pallas as pl
from jax.experimental.pallas import tpu as pltpu
from jax.sharding import PartitionSpec as P

MESH = pl.DeviceIdType.MESH
F32 = jnp.float32
BF16 = jnp.bfloat16
GROUP = 4
BLOCK = 8
WIDE = 128
PAY = 32
TOP = 8


def kernel_body(
    lat_n, lon_n, tracers, levels, rows,
    adj, cour, kern, vd, count, innov_hbm, cols_hbm,
    out, sf,
    q0, q1, fq, wind, coef, kbuf, pbuf, send, recv, a_hi, a_lo, b_hi, b_lo,
    rank_hot, tile_ref, edge, edge_e, edge_w, halo, fedge, fedge_e, fedge_w, innov, cols, obuf,
    load_sem, row_send, row_recv, col_send, col_recv, pay_send, pay_recv,
    f_send, f_recv, out_sem, own_sem,
):
    la = lax.axis_index("lat")
    lo = lax.axis_index("lon")
    me = la * lon_n + lo
    total = lat_n * lon_n
    chunks = tracers // GROUP
    parts = levels // BLOCK
    slots = kern.shape[1]
    pieces = slots // WIDE
    east = lax.rem(lo + 1, lon_n)
    west = lax.rem(lo + lon_n - 1, lon_n)

    barrier = pltpu.get_barrier_semaphore()

    @pl.loop(1, total)
    def _(i):
        p = lax.rem(me + i, total)
        pl.semaphore_signal(
            barrier, inc=1, device_id=(p // lon_n, lax.rem(p, lon_n)), device_id_type=MESH
        )

    cload = pltpu.make_async_copy(cols_hbm, cols, load_sem.at[2])
    cload.start()
    iload = pltpu.make_async_copy(innov_hbm, innov, load_sem.at[3])
    iload.start()
    kload = pltpu.make_async_copy(kern, kbuf, load_sem.at[0])
    kload.start()
    loads = []
    for g in range(chunks):
        loads.append(
            pltpu.make_async_copy(
                adj.at[pl.ds(g * GROUP, GROUP)],
                q0.at[pl.ds(g * GROUP, GROUP), :, pl.ds(TOP, rows), :],
                load_sem.at[4 + g],
            )
        )
        loads[-1].start()
    wload = pltpu.make_async_copy(cour, wind, load_sem.at[1])
    wload.start()

    cload.wait()
    col = cols[...]
    grid_cols = lon_n * 128
    grid_row = col // grid_cols
    grid_col = col - grid_row * grid_cols
    tile = (grid_row // rows) * lon_n + grid_col // 128
    cell_row = lax.rem(grid_row, rows)
    cell_col = lax.rem(grid_col, 128)
    slot = (
        lax.broadcasted_iota(jnp.int32, col.shape, 0) * 128
        + lax.broadcasted_iota(jnp.int32, col.shape, 1)
    )
    tile = jnp.where(slot < count[0], tile, -1)
    tile_ref[...] = tile
    earlier = lax.broadcasted_iota(jnp.int32, (2 * WIDE, WIDE), 0)
    later = lax.broadcasted_iota(jnp.int32, (2 * WIDE, WIDE), 1)
    adder = jnp.where((earlier <= later) | (earlier >= WIDE), 1.0, 0.0).astype(BF16)
    ids = lax.broadcasted_iota(jnp.int32, (total, WIDE), 0)
    ranks = lax.broadcasted_iota(jnp.int32, (WIDE, WIDE), 0)
    seen = jnp.zeros((total, WIDE), F32)
    for c in range(pieces):
        hot = jnp.where(ids == tile[c : c + 1, :], 1.0, 0.0)
        both = jnp.concatenate([hot.astype(BF16), seen.astype(BF16)], axis=1)
        before = jnp.dot(both, adder, preferred_element_type=F32)
        rank = jnp.sum(hot * before, axis=0, keepdims=True).astype(jnp.int32) - 1
        rank_hot[:, c * WIDE : (c + 1) * WIDE] = jnp.where(ranks == rank, 1.0, 0.0).astype(BF16)
        seen = seen + hot

    kload.wait()
    iload.wait()
    for c in range(pieces):
        spot = pl.ds(c * WIDE, WIDE)
        pbuf[0:levels, spot] = kbuf[:, spot] * innov[c : c + 1, :]
        index = lax.broadcasted_iota(jnp.int32, (PAY - levels, WIDE), 0)
        pbuf[levels:PAY, spot] = jnp.where(
            index == 0,
            cell_row[c : c + 1, :].astype(F32),
            jnp.where(index == 1, cell_col[c : c + 1, :].astype(F32), 0.0),
        )

    pl.semaphore_wait(barrier, total - 1)

    def row_copy(field, g, side, start):
        at = pl.ds(g * GROUP, GROUP)
        if side == 0:
            src, dst, to = TOP + rows - 1, TOP - 1, (la + 1, lo)
        else:
            src, dst, to = TOP, TOP + rows, (la - 1, lo)
        k = 0 if field is q0 else 1
        return pltpu.make_async_remote_copy(
            src_ref=field.at[at, :, src, :],
            dst_ref=field.at[at, :, dst, :],
            send_sem=row_send.at[k, side, g],
            recv_sem=row_recv.at[k, side, g],
            device_id=to,
            device_id_type=MESH,
        )

    has_north = la < lat_n - 1
    has_south = la > 0

    def send_rows(field, g):
        @pl.when(has_north)
        def _():
            row_copy(field, g, 0, True).start()

        @pl.when(has_south)
        def _():
            row_copy(field, g, 1, True).start()

    def arrived_rows(field, g):
        @pl.when(has_south)
        def _():
            row_copy(field, g, 0, True).wait_recv()

        @pl.when(has_north)
        def _():
            row_copy(field, g, 1, True).wait_recv()

    def sent_rows(field, g):
        @pl.when(has_north)
        def _():
            row_copy(field, g, 0, True).wait_send()

        @pl.when(has_south)
        def _():
            row_copy(field, g, 1, True).wait_send()

    for field in (q0, q1):
        @pl.when(la == 0)
        def _():
            @pl.loop(0, tracers)
            def _(t):
                field[t, :, 0:TOP, :] = jnp.zeros((levels, TOP, 128), F32)

        @pl.when(la == lat_n - 1)
        def _():
            @pl.loop(0, tracers)
            def _(t):
                field[t, :, TOP + rows :, :] = jnp.zeros((levels, TOP, 128), F32)

    @pl.when(la == 0)
    def _():
        fq[:, 0:TOP, :] = jnp.zeros((levels, TOP, 128), F32)

    @pl.when(la == lat_n - 1)
    def _():
        fq[:, TOP + rows :, :] = jnp.zeros((levels, TOP, 128), F32)

    for g in range(chunks):
        loads[g].wait()
        send_rows(q0, g)

    lane = lax.broadcasted_iota(jnp.int32, (rows, 128), 1)
    first = lane == 0
    last = lane == 127

    def col_copy(k, g, side):
        return pltpu.make_async_remote_copy(
            src_ref=edge.at[k, g],
            dst_ref=(edge_w if side == 0 else edge_e).at[k, g],
            send_sem=col_send.at[k, side, g],
            recv_sem=col_recv.at[k, side, g],
            device_id=(la, east if side == 0 else west),
            device_id_type=MESH,
        )

    def gather_edges(read, count_blocks):
        lanes = lax.broadcasted_iota(jnp.int32, (BLOCK * rows, 128), 1)
        packed = jnp.zeros((BLOCK * rows, 128), F32)
        for k in range(count_blocks):
            block = read(k).reshape(BLOCK * rows, 128)
            packed = jnp.where(lanes // 2 == k, pltpu.roll(block, (1 + 2 * k) % 128, 1), packed)
        return packed.T

    def spread(from_e, from_w):
        tall = from_e.shape[0]
        odd = lax.rem(lax.broadcasted_iota(jnp.int32, (tall, 128), 0), 2) == 1
        mixed = jnp.where(odd, pltpu.roll(from_w, 1, 0), pltpu.roll(from_e, tall - 1, 0))
        if tall < 128:
            mixed = jnp.concatenate([mixed, jnp.zeros((128 - tall, 128), F32)], axis=0)
        return mixed.T

    def send_cols(field, k, g):
        def read(b):
            return field[
                g * GROUP + b // parts,
                pl.ds((b % parts) * BLOCK, BLOCK),
                pl.ds(TOP, rows),
                :,
            ]

        edge[k, g] = gather_edges(read, GROUP * parts)[: edge.shape[2]]
        for side in (0, 1):
            col_copy(k, g, side).start()

    @pl.loop(0, chunks)
    def _(g):
        send_cols(q0, 0, g)

    def pay_copy(p, src):
        return pltpu.make_async_remote_copy(
            src_ref=send.at[p, pl.ds(0, levels + 2)],
            dst_ref=recv.at[src, pl.ds(0, levels + 2)],
            send_sem=pay_send.at[p],
            recv_sem=pay_recv.at[src],
            device_id=(p // lon_n, lax.rem(p, lon_n)),
            device_id_type=MESH,
        )

    own = pltpu.make_async_copy(send.at[me], recv.at[me], own_sem.at[0])

    @pl.loop(0, lat_n)
    def _(step):
        row = lax.rem(la + 1 + step, lat_n)

        for c in range(pieces):
            spot = pl.ds(c * WIDE, WIDE)
            block = pbuf[:, spot]
            hi = block.astype(BF16).astype(F32)
            low = block - hi
            where_to = jnp.broadcast_to(tile_ref[c : c + 1, :], (PAY, WIDE)) - row * lon_n
            for d in range(lon_n):
                mine = where_to == d
                a_hi[d * PAY : (d + 1) * PAY, spot] = jnp.where(mine, hi, 0.0).astype(BF16)
                a_lo[d * PAY : (d + 1) * PAY, spot] = jnp.where(mine, low, 0.0).astype(BF16)
        contract = (((1,), (1,)), ((), ()))
        packed = lax.dot_general(
            a_hi[...], rank_hot[...], contract, preferred_element_type=F32
        ) + lax.dot_general(a_lo[...], rank_hot[...], contract, preferred_element_type=F32)
        send[pl.ds(row * lon_n, lon_n)] = packed.reshape(lon_n, PAY, WIDE)

        @pl.loop(0, lon_n)
        def _(j):
            p = row * lon_n + lax.rem(lo + 1 + j, lon_n)

            @pl.when(p != me)
            def _():
                pay_copy(p, me).start()

    own.start()

    wload.wait()

    @pl.loop(0, levels, unroll=4)
    def _(l):
        u = wind[0, l]
        v = wind[1, l]
        coef[0, l] = 0.8 - jnp.abs(u) - jnp.abs(v) - 2.0 * vd[l]
        coef[1, l] = jnp.maximum(u, 0.0) + 0.05
        coef[2, l] = jnp.maximum(-u, 0.0) + 0.05
        coef[3, l] = jnp.maximum(v, 0.0) + 0.05
        coef[4, l] = jnp.maximum(-v, 0.0) + 0.05

    def stencil(read, l, edges, k, cs):
        q = read(l, TOP)
        beside = pltpu.roll(edges, 127 - 2 * k, 1)
        e = jnp.where(last, beside, pltpu.roll(q, 127, 1))
        w = jnp.where(first, beside, pltpu.roll(q, 1, 1))
        n = read(l, TOP + 1)
        s = read(l, TOP - 1)
        up = read(min(l + 1, levels - 1) if isinstance(l, int) else jnp.minimum(l + 1, levels - 1), TOP)
        down = read(max(l - 1, 0) if isinstance(l, int) else jnp.maximum(l - 1, 0), TOP)
        c0, ce, cw, cn, cs_, cv = cs
        return (c0 * q + ce * e) + (cw * w + cn * n) + (cs_ * s + cv * (up + down))

    def coefs(l):
        return tuple(coef[i, l] for i in range(5)) + (vd[l],)

    def advance(field, k, g, write):
        arrived_rows(field, g)
        for side in (0, 1):
            col_copy(k, g, side).wait_recv()
        halo[...] = spread(edge_e[k, g], edge_w[k, g])
        for part in range(parts):
            @pl.loop(0, BLOCK // 8)
            def _(pair):
                done = []
                for near in range(8):
                    j = pair * 8 + near
                    l = part * BLOCK + j
                    cs = coefs(l)
                    edges = halo[pl.ds(pl.multiple_of(j * rows, rows), rows), :]
                    for i in range(GROUP):
                        t = g * GROUP + i

                        def read(level, r):
                            return field[t, level, pl.ds(r, rows), :]

                        done.append((i, t, l, stencil(read, l, edges, i * parts + part, cs)))
                for item in done:
                    write(*item)

    @pl.loop(0, chunks)
    def _(g):
        def write(i, t, l, value):
            q1[t, l, TOP : TOP + rows, :] = value

        advance(q0, 0, g, write)
        send_rows(q1, g)
        send_cols(q1, 1, g)

    def out_copy(g):
        at = pl.ds(g * GROUP, GROUP)
        return pltpu.make_async_copy(obuf.at[at], out.at[at], out_sem.at[g])

    @pl.loop(0, chunks)
    def _(g):
        def write(i, t, l, value):
            obuf[t, l] = value

        advance(q1, 1, g, write)
        out_copy(g).start()

    own.wait()
    tile_rows = lax.broadcasted_iota(jnp.int32, (rows, WIDE), 0)
    fq[:, TOP : TOP + rows, :] = jnp.zeros((levels, rows, 128), F32)

    @pl.loop(0, lat_n)
    def _(step):
        source_row = lax.rem(la + lat_n - 1 - step + lat_n, lat_n)

        @pl.loop(0, lon_n)
        def _(j):
            src = source_row * lon_n + j

            @pl.when(src != me)
            def _():
                pay_copy(src, src).wait_recv()

        columns = []
        for j in range(lon_n):
            block = recv[source_row * lon_n + j]
            hi = block.astype(BF16).astype(F32)
            low = block - hi
            here = tile_rows == block[levels : levels + 1, :].astype(jnp.int32)
            spot = pl.ds(j * WIDE, WIDE)
            for l in range(levels):
                b_hi[l * rows : (l + 1) * rows, spot] = jnp.where(
                    here, hi[l : l + 1, :], 0.0
                ).astype(BF16)
                b_lo[l * rows : (l + 1) * rows, spot] = jnp.where(
                    here, low[l : l + 1, :], 0.0
                ).astype(BF16)
            columns.append(
                jnp.where(
                    ranks == block[levels + 1 : levels + 2, :].astype(jnp.int32), 1.0, 0.0
                ).astype(BF16)
            )
        hot = jnp.concatenate(columns, axis=1)
        contract = (((1,), (1,)), ((), ()))
        part = lax.dot_general(
            b_hi[...], hot, contract, preferred_element_type=F32
        ) + lax.dot_general(b_lo[...], hot, contract, preferred_element_type=F32)
        fq[:, TOP : TOP + rows, :] += part.reshape(levels, rows, 128)

    def f_rows(side):
        if side == 0:
            src, dst, to = TOP + rows - 1, TOP - 1, (la + 1, lo)
        else:
            src, dst, to = TOP, TOP + rows, (la - 1, lo)
        return pltpu.make_async_remote_copy(
            src_ref=fq.at[:, src, :],
            dst_ref=fq.at[:, dst, :],
            send_sem=f_send.at[side],
            recv_sem=f_recv.at[side],
            device_id=to,
            device_id_type=MESH,
        )

    def f_cols(side):
        return pltpu.make_async_remote_copy(
            src_ref=fedge,
            dst_ref=fedge_w if side == 0 else fedge_e,
            send_sem=f_send.at[2 + side],
            recv_sem=f_recv.at[2 + side],
            device_id=(la, east if side == 0 else west),
            device_id_type=MESH,
        )

    @pl.when(has_north)
    def _():
        f_rows(0).start()

    @pl.when(has_south)
    def _():
        f_rows(1).start()

    fedge[...] = gather_edges(
        lambda b: fq[pl.ds(b * BLOCK, BLOCK), pl.ds(TOP, rows), :], parts
    )[: fedge.shape[0]]
    for side in (0, 1):
        f_cols(side).start()
    for side in (0, 1):
        f_cols(side).wait_recv()

    @pl.when(has_south)
    def _():
        f_rows(0).wait_recv()

    @pl.when(has_north)
    def _():
        f_rows(1).wait_recv()

    halo[...] = spread(fedge_e[...], fedge_w[...])
    for part in range(parts):
        done = []
        for j in range(BLOCK):
            l = part * BLOCK + j

            def read(level, r):
                return fq[level, pl.ds(r, rows), :]

            edges = halo[j * rows : (j + 1) * rows, :]
            done.append((l, stencil(read, l, edges, part, coefs(l))))
        for l, value in done:
            sf[l] = value

    @pl.loop(0, total)
    def _(p):
        @pl.when(p != me)
        def _():
            pay_copy(p, me).wait_send()

    @pl.loop(0, chunks)
    def _(g):
        for k, field in ((0, q0), (1, q1)):
            sent_rows(field, g)
            for side in (0, 1):
                col_copy(k, g, side).wait_send()
        out_copy(g).wait()

    @pl.when(has_north)
    def _():
        f_rows(0).wait_send()

    @pl.when(has_south)
    def _():
        f_rows(1).wait_send()

    for side in (0, 1):
        f_cols(side).wait_send()


def per_device(adjoint, courant, vert_diff, kernel, innovation, sound_col, sound_count):
    tracers, levels, rows, columns = adjoint.shape
    lat_n = lax.axis_size("lat")
    lon_n = lax.axis_size("lon")
    total = lat_n * lon_n
    slots = sound_col.shape[0]
    chunks = tracers // GROUP
    parts = levels // BLOCK
    assert columns == 128 and rows == 16 and 2 * slots // total <= WIDE
    tall = rows + 2 * TOP
    edge_rows = -(-2 * GROUP * parts // 8) * 8
    vmem = pl.BlockSpec(memory_space=pltpu.VMEM)
    smem = pl.BlockSpec(memory_space=pltpu.SMEM)
    far = pl.BlockSpec(memory_space=pltpu.HBM)
    dma = pltpu.SemaphoreType.DMA
    twice, forced = pl.pallas_call(
        functools.partial(kernel_body, lat_n, lon_n, tracers, levels, rows),
        out_shape=(
            jax.ShapeDtypeStruct(adjoint.shape, F32),
            jax.ShapeDtypeStruct((levels, rows, 128), F32),
        ),
        in_specs=[far, far, far, smem, smem, far, far],
        out_specs=(far, vmem),
        scratch_shapes=[
            pltpu.VMEM((tracers, levels, tall, 128), F32),
            pltpu.VMEM((tracers, levels, tall, 128), F32),
            pltpu.VMEM((levels, tall, 128), F32),
            pltpu.VMEM((2, levels, rows, 128), F32),
            pltpu.VMEM((5, levels, rows, 128), F32),
            pltpu.VMEM((levels, slots), F32),
            pltpu.VMEM((PAY, slots), F32),
            pltpu.VMEM((total, PAY, WIDE), F32),
            pltpu.VMEM((total, PAY, WIDE), F32),
            pltpu.VMEM((lon_n * PAY, slots), BF16),
            pltpu.VMEM((lon_n * PAY, slots), BF16),
            pltpu.VMEM((levels * rows, lon_n * WIDE), BF16),
            pltpu.VMEM((levels * rows, lon_n * WIDE), BF16),
            pltpu.VMEM((WIDE, slots), BF16),
            pltpu.VMEM((slots // 128, 128), jnp.int32),
            pltpu.VMEM((2, chunks, edge_rows, 128), F32),
            pltpu.VMEM((2, chunks, edge_rows, 128), F32),
            pltpu.VMEM((2, chunks, edge_rows, 128), F32),
            pltpu.VMEM((BLOCK * rows, 128), F32),
            pltpu.VMEM((8, 128), F32),
            pltpu.VMEM((8, 128), F32),
            pltpu.VMEM((8, 128), F32),
            pltpu.VMEM((slots // 128, 128), F32),
            pltpu.VMEM((slots // 128, 128), jnp.int32),
            pltpu.VMEM(adjoint.shape, F32),
            dma((4 + chunks,)),
            dma((2, 2, chunks)),
            dma((2, 2, chunks)),
            dma((2, 2, chunks)),
            dma((2, 2, chunks)),
            dma((total,)),
            dma((total,)),
            dma((4,)),
            dma((4,)),
            dma((chunks,)),
            dma((1,)),
        ],
        compiler_params=pltpu.CompilerParams(
            collective_id=0, has_side_effects=True, vmem_limit_bytes=62 * 1024 * 1024
        ),
    )(
        adjoint,
        courant,
        kernel,
        vert_diff,
        sound_count,
        innovation.reshape(slots // 128, 128),
        sound_col.reshape(slots // 128, 128),
    )
    return twice + forced[None]


def solution(mesh):
    placed = (
        P(None, None, "lat", "lon"),
        P(None, None, "lat", "lon"),
        P(),
        P(None, ("lat", "lon")),
        P(("lat", "lon")),
        P(("lat", "lon")),
        P(("lat", "lon")),
    )
    return jax.shard_map(
        per_device,
        mesh=mesh,
        in_specs=placed,
        out_specs=P(None, None, "lat", "lon"),
        check_vma=False,
    )
```

```python
import functools

import jax
import jax.numpy as jnp
from jax import lax
from jax.experimental import pallas as pl
from jax.experimental.pallas import tpu as pltpu
from jax.sharding import PartitionSpec as P

MESH = pl.DeviceIdType.MESH
F32 = jnp.float32
BF16 = jnp.bfloat16
GROUP = 4
BLOCK = 8
WIDE = 128
PAY = 32
TOP = 8


def kernel_body(
    lat_n, lon_n, tracers, levels, rows,
    adj, cour, kern, vd, count, innov_hbm, cols_hbm,
    out, sf,
    q0, q1, fq, wind, coef, kbuf, pbuf, send, recv, a_hi, a_lo, b_hi, b_lo,
    rank_hot, tile_ref, edge, edge_e, edge_w, halo, fedge, fedge_e, fedge_w, innov, cols, obuf,
    load_sem, row_send, row_recv, col_send, col_recv, pay_send, pay_recv,
    f_send, f_recv, out_sem, own_sem,
):
    la = lax.axis_index("lat")
    lo = lax.axis_index("lon")
    me = la * lon_n + lo
    total = lat_n * lon_n
    chunks = tracers // GROUP
    parts = levels // BLOCK
    slots = kern.shape[1]
    pieces = slots // WIDE
    east = lax.rem(lo + 1, lon_n)
    west = lax.rem(lo + lon_n - 1, lon_n)

    barrier = pltpu.get_barrier_semaphore()

    @pl.loop(1, total)
    def _(i):
        p = lax.rem(me + i, total)
        pl.semaphore_signal(
            barrier, inc=1, device_id=(p // lon_n, lax.rem(p, lon_n)), device_id_type=MESH
        )

    cload = pltpu.make_async_copy(cols_hbm, cols, load_sem.at[2])
    cload.start()
    iload = pltpu.make_async_copy(innov_hbm, innov, load_sem.at[3])
    iload.start()
    kload = pltpu.make_async_copy(kern, kbuf, load_sem.at[0])
    kload.start()
    loads = []
    for g in range(chunks):
        loads.append(
            pltpu.make_async_copy(
                adj.at[pl.ds(g * GROUP, GROUP)],
                q0.at[pl.ds(g * GROUP, GROUP), :, pl.ds(TOP, rows), :],
                load_sem.at[4 + g],
            )
        )
        loads[-1].start()
    wload = pltpu.make_async_copy(cour, wind, load_sem.at[1])
    wload.start()

    cload.wait()
    col = cols[...]
    grid_cols = lon_n * 128
    grid_row = col // grid_cols
    grid_col = col - grid_row * grid_cols
    tile = (grid_row // rows) * lon_n + grid_col // 128
    cell_row = lax.rem(grid_row, rows)
    cell_col = lax.rem(grid_col, 128)
    slot = (
        lax.broadcasted_iota(jnp.int32, col.shape, 0) * 128
        + lax.broadcasted_iota(jnp.int32, col.shape, 1)
    )
    tile = jnp.where(slot < count[0], tile, -1)
    tile_ref[...] = tile
    earlier = lax.broadcasted_iota(jnp.int32, (2 * WIDE, WIDE), 0)
    later = lax.broadcasted_iota(jnp.int32, (2 * WIDE, WIDE), 1)
    adder = jnp.where((earlier <= later) | (earlier >= WIDE), 1.0, 0.0).astype(BF16)
    ids = lax.broadcasted_iota(jnp.int32, (total, WIDE), 0)
    ranks = lax.broadcasted_iota(jnp.int32, (WIDE, WIDE), 0)
    seen = jnp.zeros((total, WIDE), F32)
    for c in range(pieces):
        hot = jnp.where(ids == tile[c : c + 1, :], 1.0, 0.0)
        both = jnp.concatenate([hot.astype(BF16), seen.astype(BF16)], axis=1)
        before = jnp.dot(both, adder, preferred_element_type=F32)
        rank = jnp.sum(hot * before, axis=0, keepdims=True).astype(jnp.int32) - 1
        rank_hot[:, c * WIDE : (c + 1) * WIDE] = jnp.where(ranks == rank, 1.0, 0.0).astype(BF16)
        seen = seen + hot

    kload.wait()
    iload.wait()
    for c in range(pieces):
        spot = pl.ds(c * WIDE, WIDE)
        pbuf[0:levels, spot] = kbuf[:, spot] * innov[c : c + 1, :]
        index = lax.broadcasted_iota(jnp.int32, (PAY - levels, WIDE), 0)
        pbuf[levels:PAY, spot] = jnp.where(
            index == 0,
            cell_row[c : c + 1, :].astype(F32),
            jnp.where(index == 1, cell_col[c : c + 1, :].astype(F32), 0.0),
        )

    pl.semaphore_wait(barrier, total - 1)

    def row_copy(field, g, side, start):
        at = pl.ds(g * GROUP, GROUP)
        if side == 0:
            src, dst, to = TOP + rows - 1, TOP - 1, (la + 1, lo)
        else:
            src, dst, to = TOP, TOP + rows, (la - 1, lo)
        k = 0 if field is q0 else 1
        return pltpu.make_async_remote_copy(
            src_ref=field.at[at, :, src, :],
            dst_ref=field.at[at, :, dst, :],
            send_sem=row_send.at[k, side, g],
            recv_sem=row_recv.at[k, side, g],
            device_id=to,
            device_id_type=MESH,
        )

    has_north = la < lat_n - 1
    has_south = la > 0

    def send_rows(field, g):
        @pl.when(has_north)
        def _():
            row_copy(field, g, 0, True).start()

        @pl.when(has_south)
        def _():
            row_copy(field, g, 1, True).start()

    def arrived_rows(field, g):
        @pl.when(has_south)
        def _():
            row_copy(field, g, 0, True).wait_recv()

        @pl.when(has_north)
        def _():
            row_copy(field, g, 1, True).wait_recv()

    def sent_rows(field, g):
        @pl.when(has_north)
        def _():
            row_copy(field, g, 0, True).wait_send()

        @pl.when(has_south)
        def _():
            row_copy(field, g, 1, True).wait_send()

    for field in (q0, q1):
        @pl.when(la == 0)
        def _():
            @pl.loop(0, tracers)
            def _(t):
                field[t, :, 0:TOP, :] = jnp.zeros((levels, TOP, 128), F32)

        @pl.when(la == lat_n - 1)
        def _():
            @pl.loop(0, tracers)
            def _(t):
                field[t, :, TOP + rows :, :] = jnp.zeros((levels, TOP, 128), F32)

    @pl.when(la == 0)
    def _():
        fq[:, 0:TOP, :] = jnp.zeros((levels, TOP, 128), F32)

    @pl.when(la == lat_n - 1)
    def _():
        fq[:, TOP + rows :, :] = jnp.zeros((levels, TOP, 128), F32)

    def pay_copy(p, src):
        return pltpu.make_async_remote_copy(
            src_ref=send.at[p, pl.ds(0, levels + 2)],
            dst_ref=recv.at[src, pl.ds(0, levels + 2)],
            send_sem=pay_send.at[p],
            recv_sem=pay_recv.at[src],
            device_id=(p // lon_n, lax.rem(p, lon_n)),
            device_id_type=MESH,
        )

    own = pltpu.make_async_copy(send.at[me], recv.at[me], own_sem.at[0])

    @pl.loop(0, lat_n)
    def _(step):
        row = lax.rem(la + 1 + step, lat_n)

        for c in range(pieces):
            spot = pl.ds(c * WIDE, WIDE)
            block = pbuf[:, spot]
            hi = block.astype(BF16).astype(F32)
            low = block - hi
            where_to = jnp.broadcast_to(tile_ref[c : c + 1, :], (PAY, WIDE)) - row * lon_n
            for d in range(lon_n):
                mine = where_to == d
                a_hi[d * PAY : (d + 1) * PAY, spot] = jnp.where(mine, hi, 0.0).astype(BF16)
                a_lo[d * PAY : (d + 1) * PAY, spot] = jnp.where(mine, low, 0.0).astype(BF16)
        contract = (((1,), (1,)), ((), ()))
        packed = lax.dot_general(
            a_hi[...], rank_hot[...], contract, preferred_element_type=F32
        ) + lax.dot_general(a_lo[...], rank_hot[...], contract, preferred_element_type=F32)
        send[pl.ds(row * lon_n, lon_n)] = packed.reshape(lon_n, PAY, WIDE)

        @pl.loop(0, lon_n)
        def _(j):
            p = row * lon_n + lax.rem(lo + 1 + j, lon_n)

            @pl.when(p != me)
            def _():
                pay_copy(p, me).start()

    own.start()

    for g in range(chunks):
        loads[g].wait()
        send_rows(q0, g)

    lane = lax.broadcasted_iota(jnp.int32, (rows, 128), 1)
    first = lane == 0
    last = lane == 127

    def col_copy(k, g, side):
        return pltpu.make_async_remote_copy(
            src_ref=edge.at[k, g],
            dst_ref=(edge_w if side == 0 else edge_e).at[k, g],
            send_sem=col_send.at[k, side, g],
            recv_sem=col_recv.at[k, side, g],
            device_id=(la, east if side == 0 else west),
            device_id_type=MESH,
        )

    def gather_edges(read, count_blocks):
        lanes = lax.broadcasted_iota(jnp.int32, (BLOCK * rows, 128), 1)
        packed = jnp.zeros((BLOCK * rows, 128), F32)
        for k in range(count_blocks):
            block = read(k).reshape(BLOCK * rows, 128)
            packed = jnp.where(lanes // 2 == k, pltpu.roll(block, (1 + 2 * k) % 128, 1), packed)
        return packed.T

    def spread(from_e, from_w):
        tall = from_e.shape[0]
        odd = lax.rem(lax.broadcasted_iota(jnp.int32, (tall, 128), 0), 2) == 1
        mixed = jnp.where(odd, pltpu.roll(from_w, 1, 0), pltpu.roll(from_e, tall - 1, 0))
        if tall < 128:
            mixed = jnp.concatenate([mixed, jnp.zeros((128 - tall, 128), F32)], axis=0)
        return mixed.T

    def send_cols(field, k, g):
        def read(b):
            return field[
                g * GROUP + b // parts,
                pl.ds((b % parts) * BLOCK, BLOCK),
                pl.ds(TOP, rows),
                :,
            ]

        edge[k, g] = gather_edges(read, GROUP * parts)[: edge.shape[2]]
        for side in (0, 1):
            col_copy(k, g, side).start()

    @pl.loop(0, chunks)
    def _(g):
        send_cols(q0, 0, g)

    wload.wait()

    @pl.loop(0, levels, unroll=4)
    def _(l):
        u = wind[0, l]
        v = wind[1, l]
        coef[0, l] = 0.8 - jnp.abs(u) - jnp.abs(v) - 2.0 * vd[l]
        coef[1, l] = jnp.maximum(u, 0.0) + 0.05
        coef[2, l] = jnp.maximum(-u, 0.0) + 0.05
        coef[3, l] = jnp.maximum(v, 0.0) + 0.05
        coef[4, l] = jnp.maximum(-v, 0.0) + 0.05

    def stencil(read, l, edges, k, cs):
        q = read(l, TOP)
        beside = pltpu.roll(edges, 127 - 2 * k, 1)
        e = jnp.where(last, beside, pltpu.roll(q, 127, 1))
        w = jnp.where(first, beside, pltpu.roll(q, 1, 1))
        n = read(l, TOP + 1)
        s = read(l, TOP - 1)
        up = read(min(l + 1, levels - 1) if isinstance(l, int) else jnp.minimum(l + 1, levels - 1), TOP)
        down = read(max(l - 1, 0) if isinstance(l, int) else jnp.maximum(l - 1, 0), TOP)
        c0, ce, cw, cn, cs_, cv = cs
        return (c0 * q + ce * e) + (cw * w + cn * n) + (cs_ * s + cv * (up + down))

    def coefs(l):
        return tuple(coef[i, l] for i in range(5)) + (vd[l],)

    def advance(field, k, g, write):
        arrived_rows(field, g)
        for side in (0, 1):
            col_copy(k, g, side).wait_recv()
        halo[...] = spread(edge_e[k, g], edge_w[k, g])
        for part in range(parts):
            @pl.loop(0, BLOCK // 8)
            def _(pair):
                done = []
                for near in range(8):
                    j = pair * 8 + near
                    l = part * BLOCK + j
                    cs = coefs(l)
                    edges = halo[pl.ds(pl.multiple_of(j * rows, rows), rows), :]
                    for i in range(GROUP):
                        t = g * GROUP + i

                        def read(level, r):
                            return field[t, level, pl.ds(r, rows), :]

                        done.append((i, t, l, stencil(read, l, edges, i * parts + part, cs)))
                for item in done:
                    write(*item)

    @pl.loop(0, chunks)
    def _(g):
        def write(i, t, l, value):
            q1[t, l, TOP : TOP + rows, :] = value

        advance(q0, 0, g, write)
        send_rows(q1, g)
        send_cols(q1, 1, g)

    def out_copy(g):
        at = pl.ds(g * GROUP, GROUP)
        return pltpu.make_async_copy(obuf.at[at], out.at[at], out_sem.at[g])

    @pl.loop(0, chunks)
    def _(g):
        def write(i, t, l, value):
            obuf[t, l] = value

        advance(q1, 1, g, write)
        out_copy(g).start()

    own.wait()
    tile_rows = lax.broadcasted_iota(jnp.int32, (rows, WIDE), 0)
    fq[:, TOP : TOP + rows, :] = jnp.zeros((levels, rows, 128), F32)

    @pl.loop(0, lat_n)
    def _(step):
        source_row = lax.rem(la + lat_n - 1 - step + lat_n, lat_n)

        @pl.loop(0, lon_n)
        def _(j):
            src = source_row * lon_n + j

            @pl.when(src != me)
            def _():
                pay_copy(src, src).wait_recv()

        columns = []
        for j in range(lon_n):
            block = recv[source_row * lon_n + j]
            hi = block.astype(BF16).astype(F32)
            low = block - hi
            here = tile_rows == block[levels : levels + 1, :].astype(jnp.int32)
            spot = pl.ds(j * WIDE, WIDE)
            for l in range(levels):
                b_hi[l * rows : (l + 1) * rows, spot] = jnp.where(
                    here, hi[l : l + 1, :], 0.0
                ).astype(BF16)
                b_lo[l * rows : (l + 1) * rows, spot] = jnp.where(
                    here, low[l : l + 1, :], 0.0
                ).astype(BF16)
            columns.append(
                jnp.where(
                    ranks == block[levels + 1 : levels + 2, :].astype(jnp.int32), 1.0, 0.0
                ).astype(BF16)
            )
        hot = jnp.concatenate(columns, axis=1)
        contract = (((1,), (1,)), ((), ()))
        part = lax.dot_general(
            b_hi[...], hot, contract, preferred_element_type=F32
        ) + lax.dot_general(b_lo[...], hot, contract, preferred_element_type=F32)
        fq[:, TOP : TOP + rows, :] += part.reshape(levels, rows, 128)

    def f_rows(side):
        if side == 0:
            src, dst, to = TOP + rows - 1, TOP - 1, (la + 1, lo)
        else:
            src, dst, to = TOP, TOP + rows, (la - 1, lo)
        return pltpu.make_async_remote_copy(
            src_ref=fq.at[:, src, :],
            dst_ref=fq.at[:, dst, :],
            send_sem=f_send.at[side],
            recv_sem=f_recv.at[side],
            device_id=to,
            device_id_type=MESH,
        )

    def f_cols(side):
        return pltpu.make_async_remote_copy(
            src_ref=fedge,
            dst_ref=fedge_w if side == 0 else fedge_e,
            send_sem=f_send.at[2 + side],
            recv_sem=f_recv.at[2 + side],
            device_id=(la, east if side == 0 else west),
            device_id_type=MESH,
        )

    @pl.when(has_north)
    def _():
        f_rows(0).start()

    @pl.when(has_south)
    def _():
        f_rows(1).start()

    fedge[...] = gather_edges(
        lambda b: fq[pl.ds(b * BLOCK, BLOCK), pl.ds(TOP, rows), :], parts
    )[: fedge.shape[0]]
    for side in (0, 1):
        f_cols(side).start()
    for side in (0, 1):
        f_cols(side).wait_recv()

    @pl.when(has_south)
    def _():
        f_rows(0).wait_recv()

    @pl.when(has_north)
    def _():
        f_rows(1).wait_recv()

    halo[...] = spread(fedge_e[...], fedge_w[...])
    for part in range(parts):
        done = []
        for j in range(BLOCK):
            l = part * BLOCK + j

            def read(level, r):
                return fq[level, pl.ds(r, rows), :]

            edges = halo[j * rows : (j + 1) * rows, :]
            done.append((l, stencil(read, l, edges, part, coefs(l))))
        for l, value in done:
            sf[l] = value

    @pl.loop(0, total)
    def _(p):
        @pl.when(p != me)
        def _():
            pay_copy(p, me).wait_send()

    @pl.loop(0, chunks)
    def _(g):
        for k, field in ((0, q0), (1, q1)):
            sent_rows(field, g)
            for side in (0, 1):
                col_copy(k, g, side).wait_send()
        out_copy(g).wait()

    @pl.when(has_north)
    def _():
        f_rows(0).wait_send()

    @pl.when(has_south)
    def _():
        f_rows(1).wait_send()

    for side in (0, 1):
        f_cols(side).wait_send()


def per_device(adjoint, courant, vert_diff, kernel, innovation, sound_col, sound_count):
    tracers, levels, rows, columns = adjoint.shape
    lat_n = lax.axis_size("lat")
    lon_n = lax.axis_size("lon")
    total = lat_n * lon_n
    slots = sound_col.shape[0]
    chunks = tracers // GROUP
    parts = levels // BLOCK
    assert columns == 128 and rows == 16 and 2 * slots // total <= WIDE
    tall = rows + 2 * TOP
    edge_rows = -(-2 * GROUP * parts // 8) * 8
    vmem = pl.BlockSpec(memory_space=pltpu.VMEM)
    smem = pl.BlockSpec(memory_space=pltpu.SMEM)
    far = pl.BlockSpec(memory_space=pltpu.HBM)
    dma = pltpu.SemaphoreType.DMA
    twice, forced = pl.pallas_call(
        functools.partial(kernel_body, lat_n, lon_n, tracers, levels, rows),
        out_shape=(
            jax.ShapeDtypeStruct(adjoint.shape, F32),
            jax.ShapeDtypeStruct((levels, rows, 128), F32),
        ),
        in_specs=[far, far, far, smem, smem, far, far],
        out_specs=(far, vmem),
        scratch_shapes=[
            pltpu.VMEM((tracers, levels, tall, 128), F32),
            pltpu.VMEM((tracers, levels, tall, 128), F32),
            pltpu.VMEM((levels, tall, 128), F32),
            pltpu.VMEM((2, levels, rows, 128), F32),
            pltpu.VMEM((5, levels, rows, 128), F32),
            pltpu.VMEM((levels, slots), F32),
            pltpu.VMEM((PAY, slots), F32),
            pltpu.VMEM((total, PAY, WIDE), F32),
            pltpu.VMEM((total, PAY, WIDE), F32),
            pltpu.VMEM((lon_n * PAY, slots), BF16),
            pltpu.VMEM((lon_n * PAY, slots), BF16),
            pltpu.VMEM((levels * rows, lon_n * WIDE), BF16),
            pltpu.VMEM((levels * rows, lon_n * WIDE), BF16),
            pltpu.VMEM((WIDE, slots), BF16),
            pltpu.VMEM((slots // 128, 128), jnp.int32),
            pltpu.VMEM((2, chunks, edge_rows, 128), F32),
            pltpu.VMEM((2, chunks, edge_rows, 128), F32),
            pltpu.VMEM((2, chunks, edge_rows, 128), F32),
            pltpu.VMEM((BLOCK * rows, 128), F32),
            pltpu.VMEM((8, 128), F32),
            pltpu.VMEM((8, 128), F32),
            pltpu.VMEM((8, 128), F32),
            pltpu.VMEM((slots // 128, 128), F32),
            pltpu.VMEM((slots // 128, 128), jnp.int32),
            pltpu.VMEM(adjoint.shape, F32),
            dma((4 + chunks,)),
            dma((2, 2, chunks)),
            dma((2, 2, chunks)),
            dma((2, 2, chunks)),
            dma((2, 2, chunks)),
            dma((total,)),
            dma((total,)),
            dma((4,)),
            dma((4,)),
            dma((chunks,)),
            dma((1,)),
        ],
        compiler_params=pltpu.CompilerParams(
            collective_id=0, has_side_effects=True, vmem_limit_bytes=62 * 1024 * 1024
        ),
    )(
        adjoint,
        courant,
        kernel,
        vert_diff,
        sound_count,
        innovation.reshape(slots // 128, 128),
        sound_col.reshape(slots // 128, 128),
    )
    return twice + forced[None]


def solution(mesh):
    placed = (
        P(None, None, "lat", "lon"),
        P(None, None, "lat", "lon"),
        P(),
        P(None, ("lat", "lon")),
        P(("lat", "lon")),
        P(("lat", "lon")),
        P(("lat", "lon")),
    )
    return jax.shard_map(
        per_device,
        mesh=mesh,
        in_specs=placed,
        out_specs=P(None, None, "lat", "lon"),
        check_vma=False,
    )
```
